32 devices in a mesh: grp: 4 (over y, x), seq: 8 (over z, core).
Axes of the slice: x: 2, y: 2, z: 4, core: 2. Of those that a mesh axis runs over, the one named last changes fastest.
Arguments:
- tokens: bfloat16 [128, 1024], P(('grp', 'seq')), may hold values from -6 to 6
- attn_gain: float32 [1024], replicated, may hold values from 0.1 to 1.9
- w_qkv: bfloat16 [1024, 3072], replicated, may hold values from -0.1875 to 0.1875
- w_out: bfloat16 [1024, 1024], replicated, may hold values from -0.1875 to 0.1875
- mlp_gain: float32 [1024], replicated, may hold values from 0.1 to 1.9
- w_gate_up: bfloat16 [2, 1024, 4096], P(None, None, 'seq'), may hold values from -0.1875 to 0.1875
- w_down: bfloat16 [4096, 1024], P('seq'), may hold values from -0.09375 to 0.09375
- kv_cache: bfloat16 [384, 2, 64, 1024], P(('grp', 'seq'))
- block_owner: int32 [384], P(('grp', 'seq')), may hold values from 0 to 31, as said below
- block_fill: int32 [384], P(('grp', 'seq')), may hold values from 0 to 64, as said below
Outputs:
- output: bfloat16 [128, 1024], P(('grp', 'seq'))
The draws below stay inside these ranges and needn't reach their ends.
Inputs may be any that keep to these rules, and one draw needn't show every extreme that they name: `block_fill`: each request has at least one block; in each group one request fills exactly 32 whole blocks, every other has at most 2 blocks; blocks of one request are live from their start and all but its last are full; blocks with no live token exist in every group. `block_owner`: every served request number of a group names some block of that group.
All inputs are finite; a program needn't handle non-finite values.
Results may differ from the reference program's by a relative error of at most 0.024.
Values may be sent and summed in bfloat16 or wider, within the bound.
A program may use at most 320 MiB of HBM per device.

```python
import jax
import jax.numpy as jnp
from jax import lax

D = 1024
HEADS = 16
HD = 64
FF = 4096
BLK = 64
REQ_DEV = 4
GROUPS = 4
SHARDS = 8
REQ_GRP = 32
REQUESTS = 128
NBLOCKS = 96
LONG_BLOCKS = 32
SHORT_BLOCKS = 2


def block_layout(key):
    base_key = jax.random.fold_in(key, 7)

    def one_group(group_key):
        k_count, k_long, k_tail, k_order = jax.random.split(group_key, 4)
        requests = jnp.arange(REQ_GRP, dtype=jnp.int32)
        counts = jax.random.randint(k_count, (REQ_GRP,), 1, SHORT_BLOCKS + 1)
        longest = jax.random.randint(k_long, (), 0, REQ_GRP)
        counts = jnp.where(requests == longest, LONG_BLOCKS, counts).astype(jnp.int32)
        tail_fill = jax.random.randint(k_tail, (REQ_GRP,), 1, BLK + 1)
        tail_fill = jnp.where(requests == longest, BLK, tail_fill).astype(jnp.int32)
        end_slots = jnp.cumsum(counts).astype(jnp.int32)
        slot_ids = jnp.arange(NBLOCKS, dtype=jnp.int32)
        owners = jnp.minimum(jnp.searchsorted(end_slots, slot_ids, side='right'), REQ_GRP - 1).astype(jnp.int32)
        is_used = slot_ids < end_slots[REQ_GRP - 1]
        is_last = slot_ids == jnp.take(end_slots, owners) - 1
        filled = jnp.where(is_used, jnp.where(is_last, jnp.take(tail_fill, owners), BLK), 0).astype(jnp.int32)
        owners = jnp.where(is_used, owners, slot_ids % REQ_GRP).astype(jnp.int32)
        shuffle = jax.random.permutation(k_order, NBLOCKS)
        return (jnp.take(owners, shuffle), jnp.take(filled, shuffle))
    group_keys = jax.vmap(lambda group_index: jax.random.fold_in(base_key, group_index))(jnp.arange(GROUPS))
    owners, filled = jax.vmap(one_group)(group_keys)
    return (owners.reshape(-1).astype(jnp.int32), filled.reshape(-1).astype(jnp.int32))


def draw_block_owner(key, part):
    return block_layout(key)[0]


def draw_block_fill(key, part):
    return block_layout(key)[1]


def draw_kv_cache(key, part):
    full_shape = (GROUPS * NBLOCKS, 2, BLK, D)
    values = jnp.clip(jax.random.normal(key, full_shape, jnp.float32), -6.0, 6.0)
    return values.astype(jnp.bfloat16)


def steps_of(key, extent, cuts, least, largest):
    def one(dim, shards_of):
        heights = jax.random.uniform(jax.random.fold_in(jax.random.fold_in(key, 6), dim), (shards_of,), jnp.float32, least / len(cuts), largest / len(cuts))
        return jnp.repeat(jnp.exp(heights), extent[dim] // shards_of).reshape((-1,) + (1,) * (len(extent) - dim - 1))

    factor_of = one(*cuts[0])
    for cut in cuts[1:]:
        factor_of = factor_of * one(*cut)
    return factor_of


def centred(stream_key, dims, deviation, most, cuts=(), held_as=jnp.bfloat16):
    array = jax.random.normal(stream_key, dims, jnp.float32) * deviation
    if len(cuts) > 0:
        array = steps_of(stream_key, dims, cuts, -0.22, 0.18) * array
    return jnp.clip(array, min=-most, max=most).astype(held_as)


def setup_inputs(seed: int = 0) -> dict:
    key_of = jax.random.split(jax.random.key(seed), 11)
    tokens = centred(key_of[0], (REQUESTS, D), 1.0, 6.0, ((0, 32),))
    attn_gain = jnp.clip(1.0 + 0.18 * jax.random.normal(key_of[1], (D,), jnp.float32), 0.1, 1.9)
    w_qkv = centred(key_of[2], (D, 3 * D), D ** -0.5, 0.1875)
    w_out = centred(key_of[3], (D, D), D ** -0.5, 0.1875)
    mlp_gain = jnp.clip(1.0 + 0.18 * jax.random.normal(key_of[4], (D,), jnp.float32), 0.1, 1.9)
    w_gate_up = centred(key_of[5], (2, D, FF), D ** -0.5, 0.1875, ((2, 8),))
    w_down = centred(key_of[6], (FF, D), FF ** -0.5, 0.09375, ((0, 8),))
    kv_cache = draw_kv_cache(jax.random.fold_in(key_of[10], 71), 0)
    block_owner = draw_block_owner(jax.random.fold_in(key_of[10], 71), 0)
    block_fill = draw_block_fill(jax.random.fold_in(key_of[10], 71), 0)
    return dict(tokens=tokens, attn_gain=attn_gain, w_qkv=w_qkv, w_out=w_out, mlp_gain=mlp_gain, w_gate_up=w_gate_up, w_down=w_down, kv_cache=kv_cache, block_owner=block_owner, block_fill=block_fill)


floor_score = -1e+30
epsilon = 1e-05

def rms_scaled(row_data, gain):
    values = row_data.astype(jnp.float32)
    return values * lax.rsqrt(lax.optimization_barrier(jnp.mean(values * values, axis=-1, keepdims=True)) + epsilon) * gain

def served_rows(group_id):
    slot_ids = jnp.arange(REQ_GRP, dtype=jnp.int32)
    return (slot_ids % GROUPS * SHARDS + slot_ids // REQ_DEV) * REQ_DEV + slot_ids % REQ_DEV // GROUPS * GROUPS + group_id

def reference(tokens, attn_gain, w_qkv, w_out, mlp_gain, w_gate_up, w_down, kv_cache, block_owner, block_fill):
    normed = rms_scaled(tokens, attn_gain).astype(jnp.bfloat16)
    qkv = jnp.dot(normed, w_qkv, preferred_element_type=jnp.float32).astype(jnp.bfloat16)
    query = qkv[:, :D]
    key_new = qkv[:, D:2 * D]
    value_new = qkv[:, 2 * D:]
    served_order = jax.vmap(served_rows)(jnp.arange(GROUPS, dtype=jnp.int32))
    caches = kv_cache.reshape(GROUPS, NBLOCKS, 2, BLK, D)
    owners = block_owner.reshape(GROUPS, NBLOCKS).astype(jnp.int32)
    fills = block_fill.reshape(GROUPS, NBLOCKS).astype(jnp.int32)
    score_scale = HD ** (-0.5)

    def attend(inputs):
        row_index, group_cache, owner_ids, filled = inputs
        query_rows = query[row_index].astype(jnp.float32).reshape(REQ_GRP, HEADS, HD)
        key_rows = key_new[row_index].astype(jnp.float32).reshape(REQ_GRP, HEADS, HD)
        value_rows = value_new[row_index].astype(jnp.float32).reshape(REQ_GRP, HEADS, HD)
        key_block = group_cache[:, 0].astype(jnp.float32).reshape(NBLOCKS, BLK, HEADS, HD)
        value_block = group_cache[:, 1].astype(jnp.float32).reshape(NBLOCKS, BLK, HEADS, HD)
        scores = jnp.einsum('bhd,bthd->bht', query_rows[owner_ids], key_block) * score_scale
        is_valid = jnp.arange(BLK, dtype=jnp.int32)[None, None, :] < filled[:, None, None]
        masked = jnp.where(is_valid, scores, floor_score)
        block_max = lax.optimization_barrier(jnp.max(masked, axis=2))
        rounded = lax.optimization_barrier(jnp.where(is_valid, jnp.exp(masked - block_max[:, :, None]), 0.0).astype(jnp.bfloat16))
        weights = rounded.astype(jnp.float32)
        block_total = lax.optimization_barrier(jnp.sum(weights, axis=2))
        block_sum = jnp.einsum('bht,bthd->bhd', weights, value_block)
        own_score = lax.optimization_barrier(jnp.sum(query_rows * key_rows, axis=2)) * score_scale
        maxima = jnp.maximum(jax.ops.segment_max(block_max, owner_ids, num_segments=REQ_GRP), own_score)
        factor = jnp.exp(block_max - maxima[owner_ids])
        own_weight = jnp.exp(own_score - maxima)
        totals = jax.ops.segment_sum(block_total * factor, owner_ids, num_segments=REQ_GRP) + own_weight
        weighted = jax.ops.segment_sum(block_sum * factor[:, :, None], owner_ids, num_segments=REQ_GRP) + value_rows * own_weight[:, :, None]
        return (weighted / totals[:, :, None]).reshape(REQ_GRP, D).astype(jnp.bfloat16)
    contexts = lax.map(attend, (served_order, caches, owners, fills))
    context = jnp.zeros((REQUESTS, D), jnp.bfloat16).at[served_order.reshape(-1)].set(contexts.reshape(-1, D))
    mixed_rows = tokens.astype(jnp.float32) + jnp.dot(context, w_out, preferred_element_type=jnp.float32)
    normed_mlp = rms_scaled(mixed_rows, mlp_gain).astype(jnp.bfloat16)
    gate_part = jnp.dot(normed_mlp, w_gate_up[0], preferred_element_type=jnp.float32)
    up_part = jnp.dot(normed_mlp, w_gate_up[1], preferred_element_type=jnp.float32)
    hidden = (jax.nn.silu(gate_part) * up_part).astype(jnp.bfloat16)
    return (mixed_rows + jnp.dot(hidden, w_down, preferred_element_type=jnp.float32)).astype(jnp.bfloat16)
```

```python
import functools

import jax
import jax.numpy as jnp
from jax import lax
from jax.experimental import pallas as pl
from jax.experimental.pallas import tpu as pltpu
from jax.sharding import PartitionSpec as P

HEADS = 16
floor_score = -1e30
epsilon = 1e-05
MESH = pl.DeviceIdType.MESH
f32 = jnp.float32
bf16 = jnp.bfloat16


def iota(shape, dim):
    return lax.broadcasted_iota(jnp.int32, shape, dim)


def kernel(
    groups, shards,
    tokens, attn_gain, w_qkv, w_out, mlp_gain, w_gate_up, w_down, kv_cache, owner, fill,
    out_ref,
    wq, wkv, wo, wgu, wd, kc, vc,
    tok_rows, tok_all, stat_out, stat_in, part, merged, rows_all, lhs, down, home, total,
    load_sem, send_sem, recv_sem,
):
    g = lax.axis_index("grp")
    s = lax.axis_index("seq")
    width = tokens.shape[1]
    head_dim = width // HEADS
    quarter = width // 4
    chunks = width // 128
    devices = groups * shards
    rows = groups * shards
    blocks, _, span, _ = kv_cache.shape
    lanes = 256
    scale = head_dim ** (-0.5)

    loads = [
        pltpu.make_async_copy(w_qkv.at[:, pl.ds(0, width)], wq, load_sem.at[0]),
        pltpu.make_async_copy(kv_cache.at[:, 0], kc, load_sem.at[1]),
        pltpu.make_async_copy(kv_cache.at[:, 1], vc, load_sem.at[2]),
        pltpu.make_async_copy(w_qkv.at[:, pl.ds(width, 2 * width)], wkv, load_sem.at[3]),
        pltpu.make_async_copy(w_out, wo, load_sem.at[4]),
        pltpu.make_async_copy(w_gate_up, wgu, load_sem.at[5]),
        pltpu.make_async_copy(w_down, wd, load_sem.at[6]),
    ]

    barrier = pltpu.get_barrier_semaphore()

    to_groups = [g] + [lax.rem(g + i, groups) for i in range(1, groups)]

    def each_device(act):
        def at(step, carry):
            to_shard = lax.rem(s + step, shards)
            for to_group in to_groups:
                act(to_group, to_shard)
            return carry

        lax.fori_loop(1, shards, at, 0)
        for to_group in to_groups[1:]:
            act(to_group, s)

    def each_shard(act):
        if shards <= 8:
            for step in range(1, shards):
                act(lax.rem(s + step, shards))
            return

        def at(step, carry):
            act(lax.rem(s + step, shards))
            return carry

        lax.fori_loop(1, shards, at, 0)

    def greet(to_group, to_shard):
        pl.semaphore_signal(
            barrier, inc=1, device_id=(to_group, to_shard), device_id_type=MESH
        )

    each_device(greet)
    for load in loads:
        load.start()
    mine = tokens[...].astype(f32)
    for k in range(chunks):
        tok_rows[pl.ds(k, groups, stride=chunks), :] = mine[:, 128 * k : 128 * (k + 1)]
    pl.semaphore_wait(barrier, devices - 1)

    def tile(index):
        return pl.ds(pl.multiple_of(index * chunks, chunks), chunks)

    def drain(ref, sem):
        pltpu.make_async_copy(ref, ref, sem).wait()

    def send_token(to_group, to_shard):
        pltpu.make_async_remote_copy(
            src_ref=tok_rows.at[tile(to_group)],
            dst_ref=tok_all.at[tile(s * groups + g)],
            send_sem=send_sem.at[0], recv_sem=recv_sem.at[0],
            device_id=(to_group, to_shard), device_id_type=MESH,
        ).start()

    each_device(send_token)
    tok_all[tile(s * groups + g), :] = tok_rows[tile(g), :]

    lane_block = lax.div(iota((1, lanes), 1), HEADS)
    lane_owner = jnp.full((1, lanes), -1, jnp.int32)
    lane_fill = jnp.zeros((1, lanes), jnp.int32)
    for b in range(blocks):
        lane_owner = jnp.where(lane_block == b, owner[b], lane_owner)
        lane_fill = jnp.where(lane_block == b, fill[b], lane_fill)
    pick = jnp.concatenate(
        [(iota((HEADS, rows), 1) == owner[b]).astype(f32) for b in range(blocks)]
        + [jnp.zeros((lanes - blocks * HEADS, rows), f32)], axis=0,
    ).astype(bf16)
    member = iota((rows, lanes), 0) == lane_owner
    head_mask = lax.div(iota((HEADS, width), 1), head_dim) == iota((HEADS, width), 0)

    everyone = tok_all.at[pl.ds(0, (devices - 1) * chunks)]
    drain(everyone, recv_sem.at[0])
    x = jnp.concatenate(
        [tok_all[pl.ds(k, rows, stride=chunks), :] for k in range(chunks)], axis=1
    )
    normed = (
        x * lax.rsqrt(jnp.mean(x * x, axis=-1, keepdims=True) + epsilon) * attn_gain[...]
    ).astype(bf16)
    loads[0].wait()
    query = jnp.dot(normed, wq[...], preferred_element_type=f32).astype(bf16)

    spread = jnp.dot(pick, query, preferred_element_type=f32)
    query_heads = jnp.concatenate(
        [
            jnp.where(head_mask, spread[HEADS * b : HEADS * (b + 1)], 0.0)
            for b in range(lanes // HEADS)
        ], axis=0,
    ).astype(bf16)
    loads[1].wait()
    crossed = lax.dot_general(
        kc[...].reshape(blocks * span, width), query_heads,
        (((1,), (1,)), ((), ())), preferred_element_type=f32,
    )
    scores = jnp.zeros((span, lanes), f32)
    for b in range(blocks):
        scores = jnp.where(lane_block == b, crossed[span * b : span * (b + 1)], scores)
    valid = iota((span, lanes), 0) < lane_fill
    masked = jnp.where(valid, scores * scale, floor_score)
    block_max = jnp.max(masked, axis=0, keepdims=True)
    local_max = jnp.where(member, block_max, floor_score)
    for shift in (16, 32, 64, 128):
        local_max = jnp.maximum(local_max, pltpu.roll(local_max, shift, 1))
    shared_max = jnp.max(jnp.where(member, local_max, floor_score), axis=0, keepdims=True)
    weights = jnp.where(valid, jnp.exp(masked - shared_max), 0.0)
    weights = weights.astype(bf16).astype(f32)
    local_total = jnp.where(member, jnp.sum(weights, axis=0, keepdims=True), 0.0)
    for shift in (16, 32, 64, 128):
        local_total = local_total + pltpu.roll(local_total, shift, 1)
    lane = iota((rows, 128), 1)
    stats = jnp.where(
        lane < HEADS, local_max[:, :128], jnp.where(lane < 2 * HEADS, local_total[:, :128], 0.0)
    )
    stat_low = iota((8, 128), 0) < 4
    for i in range(rows // 8):
        stat = stats[8 * i : 8 * i + 8]
        turned = pltpu.roll(stat, 4, 0)
        stat_out[2 * i] = jnp.where(stat_low, stat, turned)
        stat_out[2 * i + 1] = jnp.where(stat_low, turned, stat)

    def send_stat(to_shard):
        pltpu.make_async_remote_copy(
            src_ref=stat_out.at[to_shard], dst_ref=stat_in.at[s],
            send_sem=send_sem.at[4], recv_sem=recv_sem.at[4],
            device_id=(g, to_shard), device_id_type=MESH,
        ).start()

    each_shard(send_stat)
    stat_in[s] = stat_out[s]

    stacked = jnp.concatenate(
        [jnp.where(lax.rem(lane_block, 4) == j, weights, 0.0) for j in range(4)], axis=0
    )
    stacked = jnp.transpose(stacked).astype(bf16)
    loads[2].wait()
    products = []
    for i in range(blocks // 4):
        product = jnp.dot(
            stacked[4 * HEADS * i : 4 * HEADS * (i + 1)],
            vc[4 * i : 4 * i + 4].reshape(4 * span, width), preferred_element_type=f32,
        )
        for j in range(4):
            products.append(jnp.where(head_mask, product[HEADS * j : HEADS * (j + 1)], 0.0))
    products.append(jnp.zeros((lanes - blocks * HEADS, width), f32))
    local_sum = jnp.dot(
        member.astype(f32).astype(bf16), jnp.concatenate(products, axis=0).astype(bf16),
        preferred_element_type=f32,
    )

    is_low = iota((8, quarter), 0) < 4
    for i in range(rows // 8):
        q = [
            local_sum[8 * i : 8 * i + 8, quarter * c : quarter * (c + 1)] for c in range(4)
        ]
        for c in (0, 2):
            even = jnp.where(is_low, q[c], pltpu.roll(q[c + 1], 4, 0))
            odd = jnp.where(is_low, pltpu.roll(q[c], 4, 0), q[c + 1])
            q[c], q[c + 1] = even, odd
        part[2 * i] = jnp.concatenate([q[0], q[2]], axis=0).astype(bf16)
        part[2 * i + 1] = jnp.concatenate([q[1], q[3]], axis=0).astype(bf16)

    def send_part(to_shard):
        pltpu.make_async_remote_copy(
            src_ref=part.at[to_shard], dst_ref=merged.at[s],
            send_sem=send_sem.at[1], recv_sem=recv_sem.at[1],
            device_id=(g, to_shard), device_id_type=MESH,
        ).start()

    each_shard(send_part)
    merged[s] = part[s]

    own_rows = (iota((8, rows), 1) == s * groups + lax.rem(iota((8, rows), 0), 4)).astype(f32)
    own_rows = own_rows.astype(bf16)
    own_query = jnp.dot(own_rows, query, preferred_element_type=f32)
    own_normed = jnp.dot(own_rows, normed, preferred_element_type=f32).astype(bf16)
    own_tokens = jnp.dot(own_rows, x.astype(bf16), preferred_element_type=f32)
    loads[3].wait()
    own_kv = jnp.dot(own_normed, wkv[...], preferred_element_type=f32).astype(bf16).astype(f32)
    own_key, own_value = own_kv[:, :width], own_kv[:, width:]
    fold = (lax.div(iota((width, 128), 0), head_dim) == iota((width, 128), 1)).astype(f32)
    own_score = (
        jnp.dot(
            own_query * own_key, fold,
            precision=lax.Precision.HIGHEST, preferred_element_type=f32,
        ) * scale
    )
    value = [own_value[:, quarter * c : quarter * (c + 1)] for c in range(4)]
    own_value = jnp.concatenate(
        [jnp.where(is_low, value[0], value[1]), jnp.where(is_low, value[2], value[3])], axis=0
    )
    expand_head = lax.rem(iota((256, quarter), 0), 128)
    expand = (
        (expand_head < HEADS)
        & (lax.rem(expand_head, HEADS // 4) == lax.div(iota((256, quarter), 1), head_dim))
    ).astype(f32).astype(bf16)
    live = iota((8, 128), 1) < HEADS
    spot = iota((16, 128), 1)
    quarter_heads = (spot < HEADS) & (
        lax.div(spot, HEADS // 4) == lax.div(iota((16, 128), 0), 4)
    )

    drain(stat_in.at[pl.ds(0, shards - 1)], recv_sem.at[4])
    peak = own_score
    for i in range(shards):
        peak = jnp.maximum(peak, stat_in[i])
    own_weight = jnp.exp(own_score - peak)
    factors = []
    totals = own_weight
    for i in range(shards):
        stat = stat_in[i]
        factor = jnp.exp(stat - peak)
        totals = totals + factor * pltpu.roll(stat, 128 - HEADS, 1)
        factors.append(factor)
    factors.append(own_weight)
    inverse = 1.0 / jnp.where(live, totals, 1.0)
    gains = []
    for factor in factors:
        gain = factor * inverse
        gains.append(jnp.where(quarter_heads, jnp.concatenate([gain, gain], axis=0), 0.0))
    gains = jnp.concatenate(gains, axis=0)
    gains_high = gains.astype(bf16)
    gains_low = (gains - gains_high.astype(f32)).astype(bf16)
    gains = jnp.dot(
        jnp.concatenate([gains_high, gains_low], axis=1), expand, preferred_element_type=f32
    )
    context = own_value * gains[16 * shards :]
    loads[4].wait()
    drain(merged.at[pl.ds(0, shards - 1)], recv_sem.at[1])
    for i in range(shards):
        context = context + merged[i].astype(f32) * gains[16 * i : 16 * i + 16]
    context = context.astype(bf16)

    mixed_parts = [
        jnp.dot(
            context, wo[quarter * c : quarter * (c + 1), :], preferred_element_type=f32
        )[8 * (c // 2) : 8 * (c // 2) + 8]
        for c in range(4)
    ]
    mixed_low = mixed_parts[0] + mixed_parts[2]
    mixed_high = mixed_parts[1] + mixed_parts[3]
    mixed = mixed_low + pltpu.roll(mixed_high, 4, 0)
    mixed = own_tokens + jnp.where(iota((8, width), 0) < 4, mixed, pltpu.roll(mixed, 4, 0))
    normed_mlp = (
        mixed * lax.rsqrt(jnp.mean(mixed * mixed, axis=-1, keepdims=True) + epsilon)
        * mlp_gain[...]
    )
    value = [normed_mlp[:, quarter * c : quarter * (c + 1)] for c in range(4)]
    rows_all[s] = jnp.concatenate(
        [jnp.where(is_low, value[0], value[1]), jnp.where(is_low, value[2], value[3])], axis=0
    ).astype(bf16)

    def send_rows(to_shard):
        pltpu.make_async_remote_copy(
            src_ref=rows_all.at[s], dst_ref=rows_all.at[s],
            send_sem=send_sem.at[2], recv_sem=recv_sem.at[2],
            device_id=(g, to_shard), device_id_type=MESH,
        ).start()

    each_shard(send_rows)
    loads[5].wait()
    loads[6].wait()
    drain(rows_all.at[pl.ds(0, shards - 1)], recv_sem.at[2])
    for i in range(rows // 8):
        even, odd = rows_all[2 * i].astype(f32), rows_all[2 * i + 1].astype(f32)
        for c in (0, 2):
            first, second = even[4 * c : 4 * c + 8], odd[4 * c : 4 * c + 8]
            lhs[8 * i : 8 * i + 8, quarter * c : quarter * (c + 1)] = jnp.where(
                is_low, first, pltpu.roll(second, 4, 0)
            )
            lhs[8 * i : 8 * i + 8, quarter * (c + 1) : quarter * (c + 2)] = jnp.where(
                is_low, pltpu.roll(first, 4, 0), second
            )
    mlp_rows = lhs[...].astype(bf16)
    gate = jnp.dot(mlp_rows, wgu[0], preferred_element_type=f32)
    up = jnp.dot(mlp_rows, wgu[1], preferred_element_type=f32)
    hidden = (gate / (1.0 + jnp.exp(-gate)) * up).astype(bf16)
    partial = jnp.dot(hidden, wd[...], preferred_element_type=f32)
    residual = jnp.concatenate([mixed] * (rows // 8), axis=0)
    row_id = iota((rows, width), 0)
    partial = partial + jnp.where(lax.div(row_id, groups) == s, residual, 0.0)
    for k in range(chunks):
        down[pl.ds(k, rows, stride=chunks), :] = partial[:, 128 * k : 128 * (k + 1)]

    def send_down(to_group, to_shard):
        pltpu.make_async_remote_copy(
            src_ref=down.at[tile(to_shard * groups + to_group)],
            dst_ref=home.at[tile(g * shards + s)],
            send_sem=send_sem.at[3], recv_sem=recv_sem.at[3],
            device_id=(to_group, to_shard), device_id_type=MESH,
        ).start()

    each_device(send_down)
    home[tile(g * shards + s), :] = down[tile(s * groups + g), :]
    drain(everyone, send_sem.at[0])
    drain(stat_in.at[pl.ds(0, shards - 1)], send_sem.at[4])
    drain(merged.at[pl.ds(0, shards - 1)], send_sem.at[1])
    drain(rows_all.at[pl.ds(0, shards - 1)], send_sem.at[2])
    drain(home.at[pl.ds(0, (devices - 1) * chunks)], recv_sem.at[3])
    for j in range(groups):
        row = home[j * shards * chunks : (j * shards + 1) * chunks, :]
        for i in range(1, shards):
            at = (j * shards + i) * chunks
            row = row + home[at : at + chunks, :]
        total[j * chunks : (j + 1) * chunks, :] = row
    out_ref[...] = jnp.concatenate(
        [total[pl.ds(k, groups, stride=chunks), :] for k in range(chunks)], axis=1
    )
    drain(home.at[pl.ds(0, (devices - 1) * chunks)], send_sem.at[3])


def body(
    tokens, attn_gain, w_qkv, w_out, mlp_gain, w_gate_up, w_down, kv_cache, block_owner, block_fill
):
    groups, shards = lax.axis_size("grp"), lax.axis_size("seq")
    row_count, width = tokens.shape
    blocks, _, span, _ = kv_cache.shape
    rows = groups * shards
    chunks = width // 128
    assert row_count == groups and chunks == 8 and groups == 4 and blocks % 4 == 0
    vmem = pl.BlockSpec(memory_space=pltpu.VMEM)
    smem = pl.BlockSpec(memory_space=pltpu.SMEM)
    hbm = pl.BlockSpec(memory_space=pl.ANY)
    output = pl.pallas_call(
        functools.partial(kernel, groups, shards),
        out_shape=jax.ShapeDtypeStruct((row_count, width), f32),
        in_specs=[vmem, vmem, hbm, hbm, vmem, hbm, hbm, hbm, smem, smem],
        out_specs=vmem,
        scratch_shapes=[
            pltpu.VMEM((width, width), bf16),
            pltpu.VMEM((width, 2 * width), bf16),
            pltpu.VMEM(w_out.shape, bf16),
            pltpu.VMEM(w_gate_up.shape, bf16),
            pltpu.VMEM(w_down.shape, bf16),
            pltpu.VMEM((blocks, span, width), bf16),
            pltpu.VMEM((blocks, span, width), bf16),
            pltpu.VMEM((row_count * chunks, 128), f32),
            pltpu.VMEM((rows * chunks, 128), f32),
            pltpu.VMEM((shards, 8, 128), f32),
            pltpu.VMEM((shards, 8, 128), f32),
            pltpu.VMEM((shards, 16, width // 4), bf16),
            pltpu.VMEM((shards, 16, width // 4), bf16),
            pltpu.VMEM((shards, 16, width // 4), bf16),
            pltpu.VMEM((rows, width), f32),
            pltpu.VMEM((rows * chunks, 128), f32),
            pltpu.VMEM((rows * chunks, 128), f32),
            pltpu.VMEM((row_count * chunks, 128), f32),
            pltpu.SemaphoreType.DMA((7,)),
            pltpu.SemaphoreType.DMA((5,)),
            pltpu.SemaphoreType.DMA((5,)),
        ],
        compiler_params=pltpu.CompilerParams(
            collective_id=0, has_side_effects=True, vmem_limit_bytes=56 * 2**20
        ),
    )(
        tokens, attn_gain.reshape(1, width), w_qkv, w_out, mlp_gain.reshape(1, width),
        w_gate_up, w_down, kv_cache, block_owner, block_fill,
    )
    return output.astype(bf16)


def solution(mesh):
    in_specs = (
        P(("grp", "seq"), None),
        P(),
        P(),
        P(),
        P(),
        P(None, None, "seq"),
        P("seq", None),
        P(("grp", "seq"), None, None, None),
        P(("grp", "seq")),
        P(("grp", "seq")),
    )
    out_specs = P(("grp", "seq"), None)
    return jax.shard_map(body, mesh=mesh, in_specs=in_specs, out_specs=out_specs, check_vma=False)
```

```python
import functools

import jax
import jax.numpy as jnp
from jax import lax
from jax.experimental import pallas as pl
from jax.experimental.pallas import tpu as pltpu
from jax.sharding import PartitionSpec as P

HEADS = 16
floor_score = -1e30
epsilon = 1e-05
MESH = pl.DeviceIdType.MESH
f32 = jnp.float32
bf16 = jnp.bfloat16


def iota(shape, dim):
    return lax.broadcasted_iota(jnp.int32, shape, dim)


def kernel(
    groups, shards,
    tokens, attn_gain, w_qkv, w_out, mlp_gain, w_gate_up, w_down, kv_cache, owner, fill,
    out_ref,
    wq, wkv, wo, wgu, wd, kc, vc,
    tok_rows, tok_all, stat_all, staged, block_all, unpacked, down, home, total,
    load_sem, send_sem, recv_sem,
):
    g = lax.axis_index("grp")
    s = lax.axis_index("seq")
    width = tokens.shape[1]
    head_dim = width // HEADS
    sums = shards * kv_cache.shape[0]
    padded = -(-sums // 128) * 128
    chunks = width // 128
    devices = groups * shards
    rows = groups * shards
    blocks, _, span, _ = kv_cache.shape
    lanes = 256
    scale = head_dim ** (-0.5)

    loads = [
        pltpu.make_async_copy(w_qkv.at[:, pl.ds(0, width)], wq, load_sem.at[0]),
        pltpu.make_async_copy(kv_cache.at[:, 0], kc, load_sem.at[1]),
        pltpu.make_async_copy(kv_cache.at[:, 1], vc, load_sem.at[2]),
        pltpu.make_async_copy(w_qkv.at[:, pl.ds(width, 2 * width)], wkv, load_sem.at[3]),
        pltpu.make_async_copy(w_out, wo, load_sem.at[4]),
        pltpu.make_async_copy(w_gate_up, wgu, load_sem.at[5]),
        pltpu.make_async_copy(w_down, wd, load_sem.at[6]),
    ]

    barrier = pltpu.get_barrier_semaphore()

    to_groups = [g] + [lax.rem(g + i, groups) for i in range(1, groups)]

    def each_device(act):
        def at(step, carry):
            to_shard = lax.rem(s + step, shards)
            for to_group in to_groups:
                act(to_group, to_shard)
            return carry

        lax.fori_loop(1, shards, at, 0)
        for to_group in to_groups[1:]:
            act(to_group, s)

    def each_shard(act):
        if shards <= 8:
            for step in range(1, shards):
                act(lax.rem(s + step, shards))
            return

        def at(step, carry):
            act(lax.rem(s + step, shards))
            return carry

        lax.fori_loop(1, shards, at, 0)

    def greet(to_group, to_shard):
        pl.semaphore_signal(
            barrier, inc=1, device_id=(to_group, to_shard), device_id_type=MESH
        )

    each_device(greet)
    for load in loads[:3]:
        load.start()
    mine = tokens[...].astype(f32)
    for k in range(chunks):
        tok_rows[pl.ds(k, groups, stride=chunks), :] = mine[:, 128 * k : 128 * (k + 1)]
    pl.semaphore_wait(barrier, devices - 1)

    def tile(index):
        return pl.ds(pl.multiple_of(index * chunks, chunks), chunks)

    def drain(ref, sem):
        pltpu.make_async_copy(ref, ref, sem).wait()

    def send_token(to_group, to_shard):
        pltpu.make_async_remote_copy(
            src_ref=tok_rows.at[tile(to_group)],
            dst_ref=tok_all.at[tile(s * groups + g)],
            send_sem=send_sem.at[0], recv_sem=recv_sem.at[0],
            device_id=(to_group, to_shard), device_id_type=MESH,
        ).start()

    each_device(send_token)
    for load in loads[3:]:
        load.start()
    tok_all[tile(s * groups + g), :] = tok_rows[tile(g), :]

    lane_block = lax.div(iota((1, lanes), 1), HEADS)
    lane_owner = jnp.full((1, lanes), -1, jnp.int32)
    lane_fill = jnp.zeros((1, lanes), jnp.int32)
    for b in range(blocks):
        lane_owner = jnp.where(lane_block == b, owner[b], lane_owner)
        lane_fill = jnp.where(lane_block == b, fill[b], lane_fill)
    pick = jnp.concatenate(
        [(iota((HEADS, rows), 1) == owner[b]).astype(f32) for b in range(blocks)]
        + [jnp.zeros((lanes - blocks * HEADS, rows), f32)], axis=0,
    ).astype(bf16)
    head_mask = lax.div(iota((HEADS, width), 1), head_dim) == iota((HEADS, width), 0)

    everyone = tok_all.at[pl.ds(0, (devices - 1) * chunks)]
    drain(everyone, recv_sem.at[0])
    x = jnp.concatenate(
        [tok_all[pl.ds(k, rows, stride=chunks), :] for k in range(chunks)], axis=1
    )
    normed = (
        x * lax.rsqrt(jnp.mean(x * x, axis=-1, keepdims=True) + epsilon) * attn_gain[...]
    ).astype(bf16)
    loads[0].wait()
    query = jnp.dot(normed, wq[...], preferred_element_type=f32).astype(bf16)

    spread = jnp.dot(pick, query, preferred_element_type=f32)
    query_heads = jnp.concatenate(
        [
            jnp.where(head_mask, spread[HEADS * b : HEADS * (b + 1)], 0.0)
            for b in range(lanes // HEADS)
        ], axis=0,
    ).astype(bf16)
    loads[1].wait()
    crossed = lax.dot_general(
        kc[...].reshape(blocks * span, width), query_heads,
        (((1,), (1,)), ((), ())), preferred_element_type=f32,
    )
    scores = jnp.zeros((span, lanes), f32)
    for b in range(blocks):
        scores = jnp.where(lane_block == b, crossed[span * b : span * (b + 1)], scores)
    valid = iota((span, lanes), 0) < lane_fill
    masked = jnp.where(valid, scores * scale, floor_score)
    block_max = jnp.max(masked, axis=0, keepdims=True)
    weights = jnp.where(valid, jnp.exp(masked - block_max), 0.0)
    weights = weights.astype(bf16).astype(f32)
    block_total = jnp.sum(weights, axis=0, keepdims=True)
    line = iota((8, 128), 0)
    stat = jnp.zeros((8, 128), f32)
    for i, value in enumerate((block_max, block_total, lane_owner.astype(f32))):
        stat = jnp.where(line == 2 * i, value[:, :128], stat)
        stat = jnp.where(line == 2 * i + 1, value[:, 128:], stat)
    stat_all[tile(s), :] = stat

    def send_stat(to_shard):
        pltpu.make_async_remote_copy(
            src_ref=stat_all.at[tile(s)], dst_ref=stat_all.at[tile(s)],
            send_sem=send_sem.at[1], recv_sem=recv_sem.at[1],
            device_id=(g, to_shard), device_id_type=MESH,
        ).start()

    each_shard(send_stat)

    stacked = jnp.concatenate(
        [jnp.where(lax.rem(lane_block, 4) == j, weights, 0.0) for j in range(4)], axis=0
    )
    stacked = jnp.transpose(stacked).astype(bf16)
    loads[2].wait()
    products = []
    for i in range(blocks // 4):
        product = jnp.dot(
            stacked[4 * HEADS * i : 4 * HEADS * (i + 1)],
            vc[4 * i : 4 * i + 4].reshape(4 * span, width), preferred_element_type=f32,
        )
        for j in range(4):
            products.append(jnp.where(head_mask, product[HEADS * j : HEADS * (j + 1)], 0.0))
    products.append(jnp.zeros((lanes - blocks * HEADS, width), f32))
    gather_heads = lax.div(iota((16, lanes), 1), HEADS) == iota((16, lanes), 0)
    block_sum = jnp.dot(
        gather_heads.astype(f32).astype(bf16), jnp.concatenate(products, axis=0).astype(bf16),
        preferred_element_type=f32,
    )
    for k in range(chunks):
        staged[pl.ds(k, blocks, stride=chunks), :] = block_sum[:blocks, 128 * k : 128 * (k + 1)]
    block_all[s] = staged[...].astype(bf16)

    def send_blocks(to_shard):
        pltpu.make_async_remote_copy(
            src_ref=block_all.at[s], dst_ref=block_all.at[s],
            send_sem=send_sem.at[2], recv_sem=recv_sem.at[2],
            device_id=(g, to_shard), device_id_type=MESH,
        ).start()

    each_shard(send_blocks)

    loads[3].wait()
    new = jnp.dot(normed, wkv[...], preferred_element_type=f32).astype(bf16).astype(f32)
    fold = lax.div(iota((width, lanes), 0), head_dim) == lax.rem(iota((width, lanes), 1), HEADS)
    own_score = (
        jnp.dot(
            query.astype(f32) * new[:, :width], fold.astype(f32),
            precision=lax.Precision.HIGHEST, preferred_element_type=f32,
        ) * scale
    )
    expand = lax.rem(iota((lanes, width), 0), HEADS) == lax.div(iota((lanes, width), 1), head_dim)
    expand = expand.astype(f32).astype(bf16)
    row_of = iota((padded, lanes), 0)
    shard_of = ((row_of.astype(f32) + 0.5) * (1.0 / blocks)).astype(jnp.int32)
    block_of = row_of - blocks * shard_of
    choose = ((shard_of[:, :shards] == iota((padded, shards), 1))).astype(f32)

    drain(stat_all.at[pl.ds(0, (shards - 1) * chunks)], recv_sem.at[1])
    maxima, sizes, owners = (
        jnp.concatenate(
            [stat_all[pl.ds(2 * i + j, shards, stride=chunks), :] for j in range(2)], axis=1
        )
        for i in range(3)
    )
    row_id = iota((rows, lanes), 0).astype(f32)
    members = [row_id == owners[i : i + 1] for i in range(shards)]
    peak = jnp.full((rows, lanes), floor_score, f32)
    for i in range(shards):
        peak = jnp.maximum(peak, jnp.where(members[i], maxima[i : i + 1], floor_score))
    for shift in (16, 32, 64, 128):
        peak = jnp.maximum(peak, pltpu.roll(peak, shift, 1))
    peak = jnp.maximum(peak, own_score)
    shard_id = iota((shards, lanes), 0)
    peaks = jnp.zeros((shards, lanes), f32)
    for i in range(shards):
        found = jnp.max(jnp.where(members[i], peak, floor_score), axis=0, keepdims=True)
        peaks = jnp.where(shard_id == i, found, peaks)
    factors = jnp.exp(maxima - peaks)
    sizes = sizes * factors
    totals = jnp.zeros((rows, lanes), f32)
    for i in range(shards):
        totals = totals + jnp.where(members[i], sizes[i : i + 1], 0.0)
    for shift in (16, 32, 64, 128):
        totals = totals + pltpu.roll(totals, shift, 1)
    own_gain = jnp.exp(own_score - peak)
    inverse = 1.0 / (totals + own_gain)
    own_gain = own_gain * inverse
    inverses = jnp.zeros((shards, lanes), f32)
    for i in range(shards):
        found = jnp.sum(jnp.where(members[i], inverse, 0.0), axis=0, keepdims=True)
        inverses = jnp.where(shard_id == i, found, inverses)
    spread_gain = jnp.dot(
        choose, factors * inverses,
        precision=lax.Precision.HIGHEST, preferred_element_type=f32,
    )
    spread_owner = jnp.dot(
        choose, owners, precision=lax.Precision.HIGHEST, preferred_element_type=f32
    )
    lane_id = iota((padded, lanes), 1)
    spread_gain = jnp.where(lax.div(lane_id, HEADS) == block_of, spread_gain, 0.0)
    gains = jnp.concatenate(
        [spread_gain, jnp.where(iota((rows, lanes), 1) < HEADS, own_gain, 0.0)], axis=0
    ).astype(bf16)
    gains = jnp.dot(gains, expand, preferred_element_type=f32)
    owner_of = jnp.sum(
        jnp.where(lane_id == HEADS * block_of, spread_owner, 0.0), axis=1, keepdims=True
    )
    wide = max(128, rows)
    owned = (iota((padded, wide), 1).astype(f32) == owner_of) & (iota((padded, wide), 0) < sums)
    owned = jnp.transpose(owned.astype(f32))[:rows].astype(bf16)
    own_part = new[:, width:] * gains[padded:]
    loads[4].wait()
    drain(block_all.at[pl.ds(0, shards - 1)], recv_sem.at[2])
    unpacked[...] = block_all[...].reshape(sums * chunks, 128).astype(f32)
    arrived = jnp.concatenate(
        [unpacked[pl.ds(k, sums, stride=chunks), :] for k in range(chunks)], axis=1
    )
    arrived = (arrived * gains[:sums]).astype(bf16)
    if padded > sums:
        arrived = jnp.concatenate([arrived, jnp.zeros((padded - sums, width), bf16)], axis=0)
    context = (jnp.dot(owned, arrived, preferred_element_type=f32) + own_part).astype(bf16)
    mixed = x + jnp.dot(context, wo[...], preferred_element_type=f32)
    mlp_rows = (
        mixed * lax.rsqrt(jnp.mean(mixed * mixed, axis=-1, keepdims=True) + epsilon)
        * mlp_gain[...]
    ).astype(bf16)
    loads[5].wait()
    loads[6].wait()
    gate = jnp.dot(mlp_rows, wgu[0], preferred_element_type=f32)
    up = jnp.dot(mlp_rows, wgu[1], preferred_element_type=f32)
    hidden = (gate / (1.0 + jnp.exp(-gate)) * up).astype(bf16)
    partial = jnp.dot(hidden, wd[...], preferred_element_type=f32)
    ours = lax.div(iota((rows, width), 0), groups) == s
    partial = partial + jnp.where(ours, mixed, 0.0)
    for k in range(chunks):
        down[pl.ds(k, rows, stride=chunks), :] = partial[:, 128 * k : 128 * (k + 1)]

    def send_down(to_group, to_shard):
        pltpu.make_async_remote_copy(
            src_ref=down.at[tile(to_shard * groups + to_group)],
            dst_ref=home.at[tile(g * shards + s)],
            send_sem=send_sem.at[3], recv_sem=recv_sem.at[3],
            device_id=(to_group, to_shard), device_id_type=MESH,
        ).start()

    each_device(send_down)
    home[tile(g * shards + s), :] = down[tile(s * groups + g), :]
    drain(everyone, send_sem.at[0])
    drain(stat_all.at[pl.ds(0, (shards - 1) * chunks)], send_sem.at[1])
    drain(block_all.at[pl.ds(0, shards - 1)], send_sem.at[2])
    drain(home.at[pl.ds(0, (devices - 1) * chunks)], recv_sem.at[3])
    for j in range(groups):
        row = home[j * shards * chunks : (j * shards + 1) * chunks, :]
        for i in range(1, shards):
            at = (j * shards + i) * chunks
            row = row + home[at : at + chunks, :]
        total[j * chunks : (j + 1) * chunks, :] = row
    out_ref[...] = jnp.concatenate(
        [total[pl.ds(k, groups, stride=chunks), :] for k in range(chunks)], axis=1
    )
    drain(home.at[pl.ds(0, (devices - 1) * chunks)], send_sem.at[3])


def body(
    tokens, attn_gain, w_qkv, w_out, mlp_gain, w_gate_up, w_down, kv_cache, block_owner, block_fill
):
    groups, shards = lax.axis_size("grp"), lax.axis_size("seq")
    row_count, width = tokens.shape
    blocks, _, span, _ = kv_cache.shape
    rows = groups * shards
    chunks = width // 128
    assert row_count == groups and chunks == 8 and groups == 4 and blocks % 4 == 0
    vmem = pl.BlockSpec(memory_space=pltpu.VMEM)
    smem = pl.BlockSpec(memory_space=pltpu.SMEM)
    hbm = pl.BlockSpec(memory_space=pl.ANY)
    output = pl.pallas_call(
        functools.partial(kernel, groups, shards),
        out_shape=jax.ShapeDtypeStruct((row_count, width), f32),
        in_specs=[vmem, vmem, hbm, hbm, vmem, hbm, hbm, hbm, smem, smem],
        out_specs=vmem,
        scratch_shapes=[
            pltpu.VMEM((width, width), bf16),
            pltpu.VMEM((width, 2 * width), bf16),
            pltpu.VMEM(w_out.shape, bf16),
            pltpu.VMEM(w_gate_up.shape, bf16),
            pltpu.VMEM(w_down.shape, bf16),
            pltpu.VMEM((blocks, span, width), bf16),
            pltpu.VMEM((blocks, span, width), bf16),
            pltpu.VMEM((row_count * chunks, 128), f32),
            pltpu.VMEM((rows * chunks, 128), f32),
            pltpu.VMEM((shards * chunks, 128), f32),
            pltpu.VMEM((blocks * chunks, 128), f32),
            pltpu.VMEM((shards, blocks * chunks, 128), bf16),
            pltpu.VMEM((shards * blocks * chunks, 128), f32),
            pltpu.VMEM((rows * chunks, 128), f32),
            pltpu.VMEM((rows * chunks, 128), f32),
            pltpu.VMEM((row_count * chunks, 128), f32),
            pltpu.SemaphoreType.DMA((7,)),
            pltpu.SemaphoreType.DMA((4,)),
            pltpu.SemaphoreType.DMA((4,)),
        ],
        compiler_params=pltpu.CompilerParams(
            collective_id=0, has_side_effects=True, vmem_limit_bytes=56 * 2**20
        ),
    )(
        tokens, attn_gain.reshape(1, width), w_qkv, w_out, mlp_gain.reshape(1, width),
        w_gate_up, w_down, kv_cache, block_owner, block_fill,
    )
    return output.astype(bf16)


def solution(mesh):
    in_specs = (
        P(("grp", "seq"), None),
        P(),
        P(),
        P(),
        P(),
        P(None, None, "seq"),
        P("seq", None),
        P(("grp", "seq"), None, None, None),
        P(("grp", "seq")),
        P(("grp", "seq")),
    )
    out_specs = P(("grp", "seq"), None)
    return jax.shard_map(body, mesh=mesh, in_specs=in_specs, out_specs=out_specs, check_vma=False)
```

```python
import functools

import jax
import jax.numpy as jnp
from jax import lax
from jax.experimental import pallas as pl
from jax.experimental.pallas import tpu as pltpu
from jax.sharding import PartitionSpec as P

HEADS = 16
floor_score = -1e30
epsilon = 1e-05
MESH = pl.DeviceIdType.MESH
f32 = jnp.float32
bf16 = jnp.bfloat16


def iota(shape, dim):
    return lax.broadcasted_iota(jnp.int32, shape, dim)


def kernel(
    groups, shards,
    tokens, attn_gain, w_qkv, w_out, mlp_gain, w_gate_up, w_down, kv_cache, owner, fill,
    out_ref,
    wq, wkv, wo, wgu, wd, kc, vc,
    tok_rows, tok_all, stat_all, staged, block_all, unpacked, wide_rows, down, home, total,
    load_sem, send_sem, recv_sem,
):
    g = lax.axis_index("grp")
    s = lax.axis_index("seq")
    width = tokens.shape[1]
    head_dim = width // HEADS
    sums = shards * kv_cache.shape[0]
    padded = -(-sums // 128) * 128
    chunks = width // 128
    devices = groups * shards
    rows = groups * shards
    blocks, _, span, _ = kv_cache.shape
    lanes = 256
    scale = head_dim ** (-0.5)

    loads = [
        pltpu.make_async_copy(w_qkv.at[:, pl.ds(0, width)], wq, load_sem.at[0]),
        pltpu.make_async_copy(kv_cache.at[:, 0], kc, load_sem.at[1]),
        pltpu.make_async_copy(kv_cache.at[:, 1], vc, load_sem.at[2]),
        pltpu.make_async_copy(w_qkv.at[:, pl.ds(width, 2 * width)], wkv, load_sem.at[3]),
        pltpu.make_async_copy(w_out, wo, load_sem.at[4]),
        pltpu.make_async_copy(w_gate_up, wgu, load_sem.at[5]),
        pltpu.make_async_copy(w_down, wd, load_sem.at[6]),
    ]

    barrier = pltpu.get_barrier_semaphore()

    to_groups = [g] + [lax.rem(g + i, groups) for i in range(1, groups)]

    def each_device(act):
        if shards <= 8:
            for step in range(shards):
                to_shard = lax.rem(s + step, shards)
                for to_group in to_groups[0 if step else 1 :]:
                    act(to_group, to_shard)
            return

        def at(step, carry):
            to_shard = lax.rem(s + step, shards)
            for to_group in to_groups:
                act(to_group, to_shard)
            return carry

        lax.fori_loop(1, shards, at, 0)
        for to_group in to_groups[1:]:
            act(to_group, s)

    def each_shard(act):
        if shards <= 8:
            for step in range(1, shards):
                act(lax.rem(s + step, shards))
            return

        def at(step, carry):
            act(lax.rem(s + step, shards))
            return carry

        lax.fori_loop(1, shards, at, 0)

    def greet(to_group, to_shard):
        pl.semaphore_signal(
            barrier, inc=1, device_id=(to_group, to_shard), device_id_type=MESH
        )

    each_device(greet)
    for load in loads[:3]:
        load.start()
    mine = tokens[...].astype(f32)
    for k in range(chunks):
        total[pl.ds(k, groups, stride=chunks), :] = mine[:, 128 * k : 128 * (k + 1)]
    tok_rows[...] = total[...].reshape(groups, chunks, 128).astype(bf16)
    pl.semaphore_wait(barrier, devices - 1)

    def tile(index):
        return pl.ds(pl.multiple_of(index * chunks, chunks), chunks)

    def drain(ref, sem):
        pltpu.make_async_copy(ref, ref, sem).wait()

    def send_token(to_group, to_shard):
        pltpu.make_async_remote_copy(
            src_ref=tok_rows.at[to_group],
            dst_ref=tok_all.at[s * groups + g],
            send_sem=send_sem.at[0], recv_sem=recv_sem.at[0],
            device_id=(to_group, to_shard), device_id_type=MESH,
        ).start()

    each_device(send_token)
    for load in loads[3:]:
        load.start()
    tok_all[s * groups + g] = tok_rows[g]

    lane_block = lax.div(iota((1, lanes), 1), HEADS)
    lane_owner = jnp.full((1, lanes), -1, jnp.int32)
    lane_fill = jnp.zeros((1, lanes), jnp.int32)
    for b in range(blocks):
        lane_owner = jnp.where(lane_block == b, owner[b], lane_owner)
        lane_fill = jnp.where(lane_block == b, fill[b], lane_fill)
    pick = jnp.concatenate(
        [(iota((HEADS, rows), 1) == owner[b]).astype(f32) for b in range(blocks)]
        + [jnp.zeros((lanes - blocks * HEADS, rows), f32)], axis=0,
    ).astype(bf16)
    head_mask = lax.div(iota((HEADS, width), 1), head_dim) == iota((HEADS, width), 0)

    everyone = tok_all.at[pl.ds(0, devices - 1)]
    drain(everyone, recv_sem.at[0])
    wide_rows[...] = tok_all[...].astype(f32).reshape(rows * chunks, 128)
    x = jnp.concatenate(
        [wide_rows[pl.ds(k, rows, stride=chunks), :] for k in range(chunks)], axis=1
    )
    normed = (
        x * lax.rsqrt(jnp.mean(x * x, axis=-1, keepdims=True) + epsilon) * attn_gain[...]
    ).astype(bf16)
    loads[0].wait()
    query = jnp.dot(normed, wq[...], preferred_element_type=f32).astype(bf16)

    spread = jnp.dot(pick, query, preferred_element_type=f32)
    query_heads = jnp.concatenate(
        [
            jnp.where(head_mask, spread[HEADS * b : HEADS * (b + 1)], 0.0)
            for b in range(lanes // HEADS)
        ], axis=0,
    ).astype(bf16)
    loads[1].wait()
    crossed = lax.dot_general(
        kc[...].reshape(blocks * span, width), query_heads,
        (((1,), (1,)), ((), ())), preferred_element_type=f32,
    )
    scores = jnp.zeros((span, lanes), f32)
    for b in range(blocks):
        scores = jnp.where(lane_block == b, crossed[span * b : span * (b + 1)], scores)
    valid = iota((span, lanes), 0) < lane_fill
    masked = jnp.where(valid, scores * scale, floor_score)
    block_max = jnp.max(masked, axis=0, keepdims=True)
    weights = jnp.where(valid, jnp.exp(masked - block_max), 0.0)
    weights = weights.astype(bf16).astype(f32)
    block_total = jnp.sum(weights, axis=0, keepdims=True)
    line = iota((8, 128), 0)
    stat = jnp.zeros((8, 128), f32)
    for i, value in enumerate((block_max, block_total, lane_owner.astype(f32))):
        stat = jnp.where(line == 2 * i, value[:, :128], stat)
        stat = jnp.where(line == 2 * i + 1, value[:, 128:], stat)
    stat_all[tile(s), :] = stat

    def send_stat(to_shard):
        pltpu.make_async_remote_copy(
            src_ref=stat_all.at[tile(s)], dst_ref=stat_all.at[tile(s)],
            send_sem=send_sem.at[1], recv_sem=recv_sem.at[1],
            device_id=(g, to_shard), device_id_type=MESH,
        ).start()

    each_shard(send_stat)

    stacked = jnp.concatenate(
        [jnp.where(lax.rem(lane_block, 4) == j, weights, 0.0) for j in range(4)], axis=0
    )
    stacked = jnp.transpose(stacked).astype(bf16)
    loads[2].wait()
    products = []
    for i in range(blocks // 4):
        product = jnp.dot(
            stacked[4 * HEADS * i : 4 * HEADS * (i + 1)],
            vc[4 * i : 4 * i + 4].reshape(4 * span, width), preferred_element_type=f32,
        )
        for j in range(4):
            products.append(jnp.where(head_mask, product[HEADS * j : HEADS * (j + 1)], 0.0))
    products.append(jnp.zeros((lanes - blocks * HEADS, width), f32))
    gather_heads = lax.div(iota((16, lanes), 1), HEADS) == iota((16, lanes), 0)
    block_sum = jnp.dot(
        gather_heads.astype(f32).astype(bf16), jnp.concatenate(products, axis=0).astype(bf16),
        preferred_element_type=f32,
    )
    for k in range(chunks):
        staged[pl.ds(k, blocks, stride=chunks), :] = block_sum[:blocks, 128 * k : 128 * (k + 1)]
    block_all[s] = staged[...].astype(bf16)

    def send_blocks(to_shard):
        pltpu.make_async_remote_copy(
            src_ref=block_all.at[s], dst_ref=block_all.at[s],
            send_sem=send_sem.at[2], recv_sem=recv_sem.at[2],
            device_id=(g, to_shard), device_id_type=MESH,
        ).start()

    each_shard(send_blocks)

    loads[3].wait()
    new = jnp.dot(normed, wkv[...], preferred_element_type=f32).astype(bf16).astype(f32)
    fold = lax.div(iota((width, lanes), 0), head_dim) == lax.rem(iota((width, lanes), 1), HEADS)
    own_score = (
        jnp.dot(
            query.astype(f32) * new[:, :width], fold.astype(f32),
            precision=lax.Precision.HIGHEST, preferred_element_type=f32,
        ) * scale
    )
    expand = lax.rem(iota((lanes, width), 0), HEADS) == lax.div(iota((lanes, width), 1), head_dim)
    expand = expand.astype(f32).astype(bf16)
    row_of = iota((padded, lanes), 0)
    shard_of = ((row_of.astype(f32) + 0.5) * (1.0 / blocks)).astype(jnp.int32)
    block_of = row_of - blocks * shard_of
    choose = ((shard_of[:, :shards] == iota((padded, shards), 1))).astype(f32)

    drain(stat_all.at[pl.ds(0, (shards - 1) * chunks)], recv_sem.at[1])
    maxima, sizes, owners = (
        jnp.concatenate(
            [stat_all[pl.ds(2 * i + j, shards, stride=chunks), :] for j in range(2)], axis=1
        )
        for i in range(3)
    )
    row_id = iota((rows, lanes), 0).astype(f32)
    members = [row_id == owners[i : i + 1] for i in range(shards)]
    peak = jnp.full((rows, lanes), floor_score, f32)
    for i in range(shards):
        peak = jnp.maximum(peak, jnp.where(members[i], maxima[i : i + 1], floor_score))
    for shift in (16, 32, 64, 128):
        peak = jnp.maximum(peak, pltpu.roll(peak, shift, 1))
    peak = jnp.maximum(peak, own_score)
    shard_id = iota((shards, lanes), 0)
    peaks = jnp.zeros((shards, lanes), f32)
    for i in range(shards):
        found = jnp.max(jnp.where(members[i], peak, floor_score), axis=0, keepdims=True)
        peaks = jnp.where(shard_id == i, found, peaks)
    factors = jnp.exp(maxima - peaks)
    sizes = sizes * factors
    totals = jnp.zeros((rows, lanes), f32)
    for i in range(shards):
        totals = totals + jnp.where(members[i], sizes[i : i + 1], 0.0)
    for shift in (16, 32, 64, 128):
        totals = totals + pltpu.roll(totals, shift, 1)
    own_gain = jnp.exp(own_score - peak)
    inverse = 1.0 / (totals + own_gain)
    own_gain = own_gain * inverse
    inverses = jnp.zeros((shards, lanes), f32)
    for i in range(shards):
        found = jnp.sum(jnp.where(members[i], inverse, 0.0), axis=0, keepdims=True)
        inverses = jnp.where(shard_id == i, found, inverses)
    spread_gain = jnp.dot(
        choose, factors * inverses,
        precision=lax.Precision.HIGHEST, preferred_element_type=f32,
    )
    spread_owner = jnp.dot(
        choose, owners, precision=lax.Precision.HIGHEST, preferred_element_type=f32
    )
    lane_id = iota((padded, lanes), 1)
    spread_gain = jnp.where(lax.div(lane_id, HEADS) == block_of, spread_gain, 0.0)
    gains = jnp.concatenate(
        [spread_gain, jnp.where(iota((rows, lanes), 1) < HEADS, own_gain, 0.0)], axis=0
    ).astype(bf16)
    gains = jnp.dot(gains, expand, preferred_element_type=f32)
    owner_of = jnp.sum(
        jnp.where(lane_id == HEADS * block_of, spread_owner, 0.0), axis=1, keepdims=True
    )
    wide = max(128, rows)
    owned = (iota((padded, wide), 1).astype(f32) == owner_of) & (iota((padded, wide), 0) < sums)
    owned = jnp.transpose(owned.astype(f32))[:rows].astype(bf16)
    own_part = new[:, width:] * gains[padded:]
    loads[4].wait()
    drain(block_all.at[pl.ds(0, shards - 1)], recv_sem.at[2])
    unpacked[...] = block_all[...].reshape(sums * chunks, 128).astype(f32)
    arrived = jnp.concatenate(
        [unpacked[pl.ds(k, sums, stride=chunks), :] for k in range(chunks)], axis=1
    )
    arrived = (arrived * gains[:sums]).astype(bf16)
    if padded > sums:
        arrived = jnp.concatenate([arrived, jnp.zeros((padded - sums, width), bf16)], axis=0)
    context = (jnp.dot(owned, arrived, preferred_element_type=f32) + own_part).astype(bf16)
    mixed = x + jnp.dot(context, wo[...], preferred_element_type=f32)
    mlp_rows = (
        mixed * lax.rsqrt(jnp.mean(mixed * mixed, axis=-1, keepdims=True) + epsilon)
        * mlp_gain[...]
    ).astype(bf16)
    loads[5].wait()
    loads[6].wait()
    gate = jnp.dot(mlp_rows, wgu[0], preferred_element_type=f32)
    up = jnp.dot(mlp_rows, wgu[1], preferred_element_type=f32)
    hidden = (gate / (1.0 + jnp.exp(-gate)) * up).astype(bf16)
    partial = jnp.dot(hidden, wd[...], preferred_element_type=f32)
    ours = lax.div(iota((rows, width), 0), groups) == s
    partial = partial + jnp.where(ours, mixed, 0.0)
    for k in range(chunks):
        wide_rows[pl.ds(k, rows, stride=chunks), :] = partial[:, 128 * k : 128 * (k + 1)]
    down[...] = wide_rows[...].reshape(rows, chunks, 128).astype(bf16)

    def send_down(to_group, to_shard):
        pltpu.make_async_remote_copy(
            src_ref=down.at[to_shard * groups + to_group],
            dst_ref=home.at[g * shards + s],
            send_sem=send_sem.at[3], recv_sem=recv_sem.at[3],
            device_id=(to_group, to_shard), device_id_type=MESH,
        ).start()

    each_device(send_down)
    home[g * shards + s] = down[s * groups + g]
    drain(everyone, send_sem.at[0])
    drain(stat_all.at[pl.ds(0, (shards - 1) * chunks)], send_sem.at[1])
    drain(block_all.at[pl.ds(0, shards - 1)], send_sem.at[2])
    drain(home.at[pl.ds(0, devices - 1)], recv_sem.at[3])
    for j in range(groups):
        row = home[j * shards].astype(f32)
        for i in range(1, shards):
            row = row + home[j * shards + i].astype(f32)
        total[j * chunks : (j + 1) * chunks, :] = row
    out_ref[...] = jnp.concatenate(
        [total[pl.ds(k, groups, stride=chunks), :] for k in range(chunks)], axis=1
    )
    drain(home.at[pl.ds(0, devices - 1)], send_sem.at[3])


def body(
    tokens, attn_gain, w_qkv, w_out, mlp_gain, w_gate_up, w_down, kv_cache, block_owner, block_fill
):
    groups, shards = lax.axis_size("grp"), lax.axis_size("seq")
    row_count, width = tokens.shape
    blocks, _, span, _ = kv_cache.shape
    rows = groups * shards
    chunks = width // 128
    assert row_count == groups and chunks == 8 and groups == 4 and blocks % 4 == 0
    vmem = pl.BlockSpec(memory_space=pltpu.VMEM)
    smem = pl.BlockSpec(memory_space=pltpu.SMEM)
    hbm = pl.BlockSpec(memory_space=pl.ANY)
    output = pl.pallas_call(
        functools.partial(kernel, groups, shards),
        out_shape=jax.ShapeDtypeStruct((row_count, width), f32),
        in_specs=[vmem, vmem, hbm, hbm, vmem, hbm, hbm, hbm, smem, smem],
        out_specs=vmem,
        scratch_shapes=[
            pltpu.VMEM((width, width), bf16),
            pltpu.VMEM((width, 2 * width), bf16),
            pltpu.VMEM(w_out.shape, bf16),
            pltpu.VMEM(w_gate_up.shape, bf16),
            pltpu.VMEM(w_down.shape, bf16),
            pltpu.VMEM((blocks, span, width), bf16),
            pltpu.VMEM((blocks, span, width), bf16),
            pltpu.VMEM((row_count, chunks, 128), bf16),
            pltpu.VMEM((rows, chunks, 128), bf16),
            pltpu.VMEM((shards * chunks, 128), f32),
            pltpu.VMEM((blocks * chunks, 128), f32),
            pltpu.VMEM((shards, blocks * chunks, 128), bf16),
            pltpu.VMEM((shards * blocks * chunks, 128), f32),
            pltpu.VMEM((rows * chunks, 128), f32),
            pltpu.VMEM((rows, chunks, 128), bf16),
            pltpu.VMEM((rows, chunks, 128), bf16),
            pltpu.VMEM((row_count * chunks, 128), f32),
            pltpu.SemaphoreType.DMA((7,)),
            pltpu.SemaphoreType.DMA((4,)),
            pltpu.SemaphoreType.DMA((4,)),
        ],
        compiler_params=pltpu.CompilerParams(
            collective_id=0, has_side_effects=True, vmem_limit_bytes=56 * 2**20
        ),
    )(
        tokens, attn_gain.reshape(1, width), w_qkv, w_out, mlp_gain.reshape(1, width),
        w_gate_up, w_down, kv_cache, block_owner, block_fill,
    )
    return output.astype(bf16)


def solution(mesh):
    in_specs = (
        P(("grp", "seq"), None),
        P(),
        P(),
        P(),
        P(),
        P(None, None, "seq"),
        P("seq", None),
        P(("grp", "seq"), None, None, None),
        P(("grp", "seq")),
        P(("grp", "seq")),
    )
    out_specs = P(("grp", "seq"), None)
    return jax.shard_map(body, mesh=mesh, in_specs=in_specs, out_specs=out_specs, check_vma=False)
```
